256 devices in a mesh: dp: 8 (over z_lo, core), seq: 32 (over y, x, z_hi).
Axes of the slice: x: 4, y: 4, z: 8 (z_hi: 2, z_lo: 4; z = z_hi * 4 + z_lo), core: 2. Of those that a mesh axis runs over, the one named last changes fastest.
Arguments:
- queries: bfloat16 [16, 2048, 4096], P('dp', 'seq'), may hold values from -40 to 40
- keys: bfloat16 [16, 2048, 4096], P('dp', 'seq'), may hold values from -40 to 40
- values: bfloat16 [16, 2048, 4096], P('dp', 'seq'), may hold values from -6 to 6
- out_grad: bfloat16 [16, 2048, 4096], P('dp', 'seq'), may hold values from -4400 to 4400
- q_gain: float32 [32, 128], replicated, may hold values from 0.5 to 6
- k_gain: float32 [32, 128], replicated, may hold values from 0.5 to 6
Outputs:
- q_grad: bfloat16 [16, 2048, 4096], P('dp', 'seq')
- k_grad: bfloat16 [16, 2048, 4096], P('dp', 'seq')
- v_grad: bfloat16 [16, 2048, 4096], P('dp', 'seq')
- q_gain_grad: float32 [32, 128], P('seq')
- k_gain_grad: float32 [32, 128], P('seq')
The draws below stay inside these ranges and needn't reach their ends.
All inputs are finite; a program needn't handle non-finite values.
Results may differ from the reference program's by a relative error of at most 0.004.
The reference program's roundings to bfloat16 on the way count: a program that leaves them out, or rounds other values in their place, can miss the bound.
Values may be sent and summed in bfloat16 or wider, within the bound.
A program may use at most 64 MiB of HBM per device.

```python
import math
import jax
import jax.numpy as jnp
from jax import lax

HEADS = 32
HEAD_DIM = 128
WIDTH = 4096
LEN = 2048
BATCH = 16


def spread_field(key):
    pieces = jax.random.split(key, 4)
    shape = (BATCH, LEN, HEADS, HEAD_DIM)
    gauss = jnp.clip(jax.random.normal(pieces[0], shape, jnp.float32), -4.0, 4.0)
    row_scale = jnp.exp(jax.random.uniform(pieces[2], (BATCH, LEN, HEADS, 1), jnp.float32, math.log(0.3), math.log(3.0)))
    column_scale = jnp.exp(jax.random.uniform(pieces[3], (1, 1, HEADS, HEAD_DIM), jnp.float32, math.log(0.3), math.log(3.0)))
    return gauss * row_scale * column_scale


def key_field(key):
    return spread_field(jax.random.fold_in(key, 71))


def draw_keys(key, part):
    field = key_field(key)
    return field.reshape(BATCH, LEN, HEADS * HEAD_DIM).astype(jnp.bfloat16)


def draw_queries(key, part):
    key = jax.random.fold_in(key, 5)
    field = spread_field(key)
    return field.reshape(BATCH, LEN, HEADS * HEAD_DIM).astype(jnp.bfloat16)


def draw_out_grad(key, part):
    key = jax.random.fold_in(key, 13)
    pieces = jax.random.split(key, 1)
    shape = (BATCH, LEN, HEADS * HEAD_DIM)
    position = jnp.arange(LEN).astype(jnp.float32).reshape(1, LEN, 1) / max(LEN - 1, 1)
    sample = jnp.arange(BATCH).astype(jnp.float32).reshape(BATCH, 1, 1) / max(BATCH - 1, 1)
    entries = jnp.clip(jax.random.normal(pieces[0], shape, jnp.float32), -4.0, 4.0)
    rising = jnp.power(3.0, position) * jnp.power(3.0, sample)
    return (32.0 * entries * rising).astype(jnp.bfloat16)


def gain_field(key):
    pieces = jax.random.split(key, 2)
    return jax.random.uniform(pieces[1], (HEADS, HEAD_DIM), jnp.float32, 0.6, 1.6)


def draw_q_gain(key, part):
    key = jax.random.fold_in(key, 7)
    return gain_field(key)


def draw_k_gain(key, part):
    key = jax.random.fold_in(key, 9)
    return gain_field(key)


def level_of(own_key, dims, cuts, low, largest):
    level = 1.0
    for dim, shards_of in cuts:
        heights = jax.random.uniform(jax.random.fold_in(jax.random.fold_in(own_key, 6), dim), (shards_of,), jnp.float32, low / len(cuts), largest / len(cuts))
        level = level * jnp.repeat(jnp.exp(heights), dims[dim] // shards_of).reshape((-1,) + (1,) * (len(dims) - 1 - dim))
    return level


def normal_values(own_key, shape, deviation, reach, cuts=(), kind=jnp.bfloat16):
    loudness = level_of(own_key, shape, cuts, -0.22, 0.18) if cuts else 1.0
    values = jax.random.normal(own_key, shape, jnp.float32) * deviation * loudness
    return jnp.minimum(jnp.maximum(values, -reach), reach).astype(kind)


def setup_inputs(seed: int = 0) -> dict:
    splits = jax.random.split(jax.random.key(seed), 7)
    return {
        "queries": draw_queries(jax.random.fold_in(splits[6], 71), 0),
        "keys": draw_keys(jax.random.fold_in(splits[6], 71), 0),
        "values": normal_values(splits[2], (BATCH, LEN, WIDTH), 1.0, 6.0, ((0, 8), (1, 32))),
        "out_grad": draw_out_grad(jax.random.fold_in(splits[6], 71), 0),
        "q_gain": draw_q_gain(jax.random.fold_in(splits[6], 71), 0),
        "k_gain": draw_k_gain(jax.random.fold_in(splits[6], 71), 0),
    }


def normalize(raw, gain):
    widened = raw.astype(jnp.float32)
    rate = lax.rsqrt(lax.optimization_barrier(jnp.mean(widened * widened, axis=-1, keepdims=True)) + 1e-06)
    unit = widened * rate
    return (unit, rate, (unit * gain).astype(jnp.bfloat16))

def norm_back(unit, rate, grad, gain):
    grad_wide = lax.optimization_barrier(grad).astype(jnp.float32)
    scaled = gain * grad_wide
    inner = lax.optimization_barrier(jnp.mean(scaled * unit, axis=-1, keepdims=True))
    result = (rate * (scaled - unit * inner)).astype(jnp.bfloat16)
    return (result, lax.optimization_barrier(jnp.sum(grad_wide * unit, axis=0)))

def head_grads(item):
    query_rows, key_rows, value_rows, grad_rows, query_gain, key_gain = item
    query_unit, query_rate, query_normed = normalize(query_rows, query_gain)
    key_unit, key_rate, key_normed = normalize(key_rows, key_gain)
    scale = HEAD_DIM ** (-0.5)
    scores = jnp.dot(query_normed, key_normed.T, preferred_element_type=jnp.float32) * scale
    scores = scores - lax.optimization_barrier(jnp.max(scores, axis=-1, keepdims=True))
    weights = jnp.exp(scores)
    probs = weights / lax.optimization_barrier(jnp.sum(weights, axis=-1, keepdims=True))
    probs_low = probs.astype(jnp.bfloat16)
    prob_grad = jnp.dot(grad_rows, value_rows.T, preferred_element_type=jnp.float32)
    row_dot = lax.optimization_barrier(jnp.sum(probs * prob_grad, axis=-1, keepdims=True))
    score_grad = (probs * (prob_grad - row_dot) * scale).astype(jnp.bfloat16)
    value_grad = jnp.dot(probs_low.T, grad_rows, preferred_element_type=jnp.float32).astype(jnp.bfloat16)
    query_grad = jnp.dot(score_grad, key_normed, preferred_element_type=jnp.float32).astype(jnp.bfloat16)
    key_grad = jnp.dot(score_grad.T, query_normed, preferred_element_type=jnp.float32).astype(jnp.bfloat16)
    query_back, query_term = norm_back(query_unit, query_rate, query_grad, query_gain)
    key_back, key_term = norm_back(key_unit, key_rate, key_grad, key_gain)
    return (query_back, key_back, value_grad, query_term, key_term)

def reference(queries, keys, values, out_grad, q_gain, k_gain):

    def split_heads(array):
        return array.reshape(BATCH, LEN, HEADS, HEAD_DIM).transpose(0, 2, 1, 3).reshape(BATCH * HEADS, LEN, HEAD_DIM)

    def join_heads(array):
        return array.reshape(BATCH, HEADS, LEN, HEAD_DIM).transpose(0, 2, 1, 3).reshape(BATCH, LEN, HEADS * HEAD_DIM)
    query_gains = jnp.tile(q_gain, (BATCH, 1))
    key_gains = jnp.tile(k_gain, (BATCH, 1))
    query_back, key_back, value_grad, query_term, key_term = lax.map(head_grads, (split_heads(queries), split_heads(keys), split_heads(values), split_heads(out_grad), query_gains, key_gains))
    factor = 1.0 / math.sqrt(BATCH * LEN)
    q_gain_grad = lax.optimization_barrier(jnp.sum(query_term.reshape(BATCH, HEADS, HEAD_DIM), axis=0)) * factor
    k_gain_grad = lax.optimization_barrier(jnp.sum(key_term.reshape(BATCH, HEADS, HEAD_DIM), axis=0)) * factor
    return (join_heads(query_back), join_heads(key_back), join_heads(value_grad), q_gain_grad, k_gain_grad)
```

```python
import functools, math
import jax, jax.numpy as jnp
from jax import lax
from jax.experimental import pallas as pl
from jax.experimental.pallas import tpu as pltpu

DEPTH = 128
SCALE = DEPTH ** -0.5
EXP_SCALE = SCALE * math.log2(math.e)
BQ = 256
CHUNK = 512
NT = (((1,), (1,)), ((), ()))
NN = (((1,), (0,)), ((), ()))


def dot(a, b, dims=NN):
    return lax.dot_general(a, b, dims, preferred_element_type=jnp.float32)


def unit_of(raw):
    wide = raw.astype(jnp.float32)
    rate = lax.rsqrt(jnp.mean(wide * wide, axis=-1, keepdims=True) + 1e-06)
    return wide * rate, rate


def normalize(raw_ref, gain, normed_ref, rows=256):
    @pl.loop(0, raw_ref.shape[0], step=rows)
    def _(r):
        at = pl.ds(pl.multiple_of(r, rows), rows)
        unit, _ = unit_of(raw_ref[at])
        normed_ref[at] = (unit * gain).astype(jnp.bfloat16)


def norm_back(raw, grad, gain):
    unit, rate = unit_of(raw)
    wide = grad.astype(jnp.float32)
    scaled = gain * wide
    inner = jnp.mean(scaled * unit, axis=-1, keepdims=True)
    return (rate * (scaled - unit * inner)).astype(jnp.bfloat16), jnp.sum(wide * unit, axis=0, keepdims=True)


def fold(x, op):
    rows = x.shape[0]
    out = x[:8]
    for r in range(8, rows, 8):
        out = op(out, x[r:r + 8])
    return out


def attend_block(qn, g, kn_ref, knt_ref, v_ref, w_ref, p_ref, key_acc, value_acc):
    length = kn_ref.shape[0]
    chunks = [pl.ds(c, CHUNK) for c in range(0, length, CHUNK)]
    top = None
    for at in chunks:
        s = dot(kn_ref[at], qn, NT)
        w_ref[at] = s
        part = fold(s, jnp.maximum)
        top = part if top is None else jnp.maximum(top, part)
    top = jnp.max(top, axis=0, keepdims=True) * EXP_SCALE
    total = dotted = None
    for at in chunks:
        w = jnp.exp2(w_ref[at] * EXP_SCALE - top)
        w_ref[at] = w
        p = dot(v_ref[at], g, NT)
        p_ref[at] = p
        a, b = fold(w, jnp.add), fold(w * p, jnp.add)
        total, dotted = (a, b) if total is None else (total + a, dotted + b)
    total = jnp.sum(total, axis=0, keepdims=True)
    dotted = jnp.sum(dotted, axis=0, keepdims=True)
    inverse = 1.0 / total
    row_dot = dotted * inverse
    query_t = None
    for at in chunks:
        probs = w_ref[at] * inverse
        value_acc[at] += dot(probs.astype(jnp.bfloat16), g)
        score_grad = (probs * (p_ref[at] - row_dot) * SCALE).astype(jnp.bfloat16)
        key_acc[at] += dot(score_grad, qn)
        part = dot(knt_ref[:, at], score_grad)
        query_t = part if query_t is None else query_t + part
    return query_t.T.astype(jnp.bfloat16)

from jax.sharding import PartitionSpec as P

MESH = pl.DeviceIdType.MESH
BACK_ROWS = 256


def kernel(
    seq, dps, factor,
    k_in, v_in, q_in, g_in, q_gain, k_gain,
    q_out, k_out, v_out, q_term, k_term,
    held, ready, qn, kn, knt, w, p, key_acc, value_acc, term, terms,
    there_send, there_recv, there_own, back_send, back_recv, back_own, term_send, term_recv,
):
    me, group = lax.axis_index("seq"), lax.axis_index("dp")
    ins, outs = (k_in, v_in, q_in, g_in), (q_out, k_out, v_out)
    samples, tokens, _ = q_in.shape
    length = seq * tokens
    mine = pl.ds(pl.multiple_of(me * tokens, tokens), tokens)
    my_columns = pl.ds(pl.multiple_of(me * DEPTH, DEPTH), DEPTH)

    def there(b, t, peer):
        return pltpu.make_async_remote_copy(
            src_ref=ins[t].at[b, :, pl.ds(pl.multiple_of(peer * DEPTH, DEPTH), DEPTH)],
            dst_ref=held.at[b, t, mine],
            send_sem=there_send.at[b, t], recv_sem=there_recv.at[b, t],
            device_id=(group, peer), device_id_type=MESH)

    def there_local(b, t):
        return pltpu.make_async_copy(ins[t].at[b, :, my_columns], held.at[b, t, mine], there_own.at[b, t])

    def there_all(b, t):
        rows = held.at[b, t, pl.ds(0, length - tokens)]
        return pltpu.make_async_remote_copy(
            src_ref=rows, dst_ref=rows, send_sem=there_send.at[b, t], recv_sem=there_recv.at[b, t],
            device_id=(group, me), device_id_type=MESH)

    def back(b, o, peer):
        return pltpu.make_async_remote_copy(
            src_ref=ready.at[b, o, pl.ds(pl.multiple_of(peer * tokens, tokens), tokens)],
            dst_ref=outs[o].at[b, :, my_columns],
            send_sem=back_send.at[b, o], recv_sem=back_recv.at[b, o],
            device_id=(group, peer), device_id_type=MESH)

    def back_local(b, o):
        return pltpu.make_async_copy(ready.at[b, o, mine], outs[o].at[b, :, my_columns], back_own.at[b, o])

    def back_all(b, o):
        rows = ready.at[b, o, pl.ds(0, length - tokens)]
        return pltpu.make_async_remote_copy(
            src_ref=rows, dst_ref=rows, send_sem=back_send.at[b, o], recv_sem=back_recv.at[b, o],
            device_id=(group, me), device_id_type=MESH)

    def send_back(b, o):
        back_local(b, o).start()

        @pl.loop(1, seq)
        def _(r):
            back(b, o, lax.rem(me + r, seq)).start()

    barrier = pltpu.get_barrier_semaphore()

    @pl.loop(1, seq)
    def _(r):
        pl.semaphore_signal(barrier, inc=1, device_id=(group, lax.rem(me + r, seq)), device_id_type=MESH)

    @pl.loop(1, dps)
    def _(r):
        pl.semaphore_signal(barrier, inc=1, device_id=(lax.rem(group + r, dps), me), device_id_type=MESH)

    for b in range(samples):
        for t in range(4):
            there_local(b, t).start()
    pl.semaphore_wait(barrier, seq + dps - 2)
    for b in range(samples):
        for t in range(4):
            @pl.loop(1, seq)
            def _(r):
                there(b, t, lax.rem(me + r, seq)).start()

    gain_q, gain_k = q_gain[pl.ds(me, 1)], k_gain[pl.ds(me, 1)]
    term[...] = jnp.zeros_like(term)
    for b in range(samples):
        for t in range(4):
            there_local(b, t).wait()
            there_all(b, t).wait_recv()
        keys, values, queries, grads = (held.at[b, t] for t in range(4))
        normalize(keys, gain_k, kn)
        normalize(queries, gain_q, qn)
        knt[...] = kn[...].T
        key_acc[...] = jnp.zeros_like(key_acc)
        value_acc[...] = jnp.zeros_like(value_acc)

        @pl.loop(0, length, step=BQ)
        def _(r):
            at = pl.ds(pl.multiple_of(r, BQ), BQ)
            grad = attend_block(qn[at], grads[at], kn, knt, values, w, p, key_acc, value_acc)
            result, part = norm_back(queries[at], grad, gain_q)
            ready[b, 0, at] = result
            term[0:1] += part

        send_back(b, 0)

        @pl.loop(0, length, step=BACK_ROWS)
        def _(r):
            at = pl.ds(pl.multiple_of(r, BACK_ROWS), BACK_ROWS)
            result, part = norm_back(keys[at], key_acc[at].astype(jnp.bfloat16), gain_k)
            ready[b, 1, at] = result
            term[1:2] += part
            ready[b, 2, at] = value_acc[at].astype(jnp.bfloat16)

        send_back(b, 1)
        send_back(b, 2)

    def share(r):
        return pltpu.make_async_remote_copy(
            src_ref=term, dst_ref=terms.at[r], send_sem=term_send.at[r], recv_sem=term_recv.at[r],
            device_id=(lax.rem(group + r, dps), me), device_id_type=MESH)

    for r in range(1, dps):
        share(r).start()
    for r in range(1, dps):
        share(r).wait()
    total = term[...]
    for r in range(1, dps):
        total += terms[r]
    q_term[...] = total[0:1] * factor
    k_term[...] = total[1:2] * factor
    for b in range(samples):
        for t in range(4):
            there_all(b, t).wait_send()
        for o in range(3):
            back_local(b, o).wait()
            back_all(b, o).wait()


def solution(mesh):
    seq, dps = mesh.shape["seq"], mesh.shape["dp"]

    def step(queries, keys, values, out_grad, q_gain, k_gain):
        samples, tokens, _ = queries.shape
        length = seq * tokens
        vmem, anywhere = pl.BlockSpec(memory_space=pltpu.VMEM), pl.BlockSpec(memory_space=pl.ANY)
        whole = jax.ShapeDtypeStruct(queries.shape, jnp.bfloat16)
        row = jax.ShapeDtypeStruct((1, DEPTH), jnp.float32)
        dma = pltpu.SemaphoreType.DMA
        return pl.pallas_call(
            functools.partial(kernel, seq, dps, 1.0 / math.sqrt(samples * dps * length)),
            out_shape=(whole, whole, whole, row, row),
            in_specs=[anywhere] * 4 + [vmem] * 2,
            out_specs=[anywhere] * 3 + [vmem] * 2,
            scratch_shapes=[
                pltpu.VMEM((samples, 4, length, DEPTH), jnp.bfloat16),
                pltpu.VMEM((samples, 3, length, DEPTH), jnp.bfloat16),
                pltpu.VMEM((length, DEPTH), jnp.bfloat16),
                pltpu.VMEM((length, DEPTH), jnp.bfloat16),
                pltpu.VMEM((DEPTH, length), jnp.bfloat16),
                pltpu.VMEM((length, BQ), jnp.float32),
                pltpu.VMEM((length, BQ), jnp.float32),
                pltpu.VMEM((length, DEPTH), jnp.float32),
                pltpu.VMEM((length, DEPTH), jnp.float32),
                pltpu.VMEM((8, DEPTH), jnp.float32),
                pltpu.VMEM((dps, 8, DEPTH), jnp.float32),
                dma((samples, 4)), dma((samples, 4)), dma((samples, 4)),
                dma((samples, 3)), dma((samples, 3)), dma((samples, 3)),
                dma((dps,)), dma((dps,)),
            ],
            compiler_params=pltpu.CompilerParams(
                collective_id=0, has_side_effects=True, vmem_limit_bytes=48 * 2**20
            ),
        )(keys, values, queries, out_grad, q_gain, k_gain)

    return jax.shard_map(
        step,
        mesh=mesh,
        in_specs=(P("dp", "seq", None),) * 4 + (P(), P()),
        out_specs=(P("dp", "seq", None),) * 3 + (P("seq", None),) * 2,
        check_vma=False,
    )
```

```python
import functools, math
import jax, jax.numpy as jnp
from jax import lax
from jax.experimental import pallas as pl
from jax.experimental.pallas import tpu as pltpu

DEPTH = 128
SCALE = DEPTH ** -0.5
EXP_SCALE = SCALE * math.log2(math.e)
BQ = 256
CHUNK = 512
BLOCKS = 4
NT = (((1,), (1,)), ((), ()))
NN = (((1,), (0,)), ((), ()))


def dot(a, b, dims=NN):
    return lax.dot_general(a, b, dims, preferred_element_type=jnp.float32)


def unit_of(raw):
    wide = raw.astype(jnp.float32)
    rate = lax.rsqrt(jnp.mean(wide * wide, axis=-1, keepdims=True) + 1e-06)
    return wide * rate, rate


def normalize(raw_ref, gain, normed_ref, rows=256):
    @pl.loop(0, raw_ref.shape[0], step=rows)
    def _(r):
        at = pl.ds(pl.multiple_of(r, rows), rows)
        unit, _ = unit_of(raw_ref[at])
        normed_ref[at] = (unit * gain).astype(jnp.bfloat16)


def norm_back(raw, grad, gain):
    unit, rate = unit_of(raw)
    wide = grad.astype(jnp.float32)
    scaled = gain * wide
    inner = jnp.mean(scaled * unit, axis=-1, keepdims=True)
    return (rate * (scaled - unit * inner)).astype(jnp.bfloat16), jnp.sum(wide * unit, axis=0, keepdims=True)


def fold(x, op):
    rows = x.shape[0]
    out = x[:8]
    for r in range(8, rows, 8):
        out = op(out, x[r:r + 8])
    return out


from jax.sharding import PartitionSpec as P

MESH = pl.DeviceIdType.MESH


def weigh(qn, g, kn_ref, v_ref, w_ref, p_ref):
    chunks = [pl.ds(c, CHUNK) for c in range(0, kn_ref.shape[0], CHUNK)]
    top = None
    for at in chunks:
        s = dot(kn_ref[at], qn, NT)
        w_ref[at] = s
        part = fold(s, jnp.maximum)
        top = part if top is None else jnp.maximum(top, part)
    top = jnp.max(top, axis=0, keepdims=True) * EXP_SCALE
    total = dotted = None
    for at in chunks:
        w = jnp.exp2(w_ref[at] * EXP_SCALE - top)
        w_ref[at] = w
        p = dot(v_ref[at], g, NT)
        p_ref[at] = p
        a, b = fold(w, jnp.add), fold(w * p, jnp.add)
        total, dotted = (a, b) if total is None else (total + a, dotted + b)
    return top, jnp.sum(total, axis=0, keepdims=True), jnp.sum(dotted, axis=0, keepdims=True)


def gradients(qn, g, inverse, row_dot, knt_ref, w_ref, p_ref, key_acc, value_acc):
    query_t = None
    for c in range(0, w_ref.shape[0], CHUNK):
        at = pl.ds(c, CHUNK)
        probs = w_ref[at] * inverse
        value_acc[at] += dot(probs.astype(jnp.bfloat16), g)
        score_grad = (probs * (p_ref[at] - row_dot) * SCALE).astype(jnp.bfloat16)
        key_acc[at] += dot(score_grad, qn)
        part = dot(knt_ref[:, at], score_grad)
        query_t = part if query_t is None else query_t + part
    return query_t


def kernel(
    pairs, dps, factor,
    q_in, g_in, k_in, v_in, q_gain_in, k_gain_in,
    q_out, k_out, v_out, q_term, k_term,
    held, kept, ready, qn, kn, knt, w, p, key_acc, value_acc, own_part, part, their_part, stats, their_stats, term, terms,
    q_gain, k_gain, gain_sem, there_send, there_recv, kept_send, kept_recv, own_sem, back_send, back_recv, back_own,
    part_send, part_recv, stats_send, stats_recv, term_send, term_recv,
):
    me, group = lax.axis_index("seq"), lax.axis_index("dp")
    j, half = me // 2, lax.rem(me, 2)
    other = 1 - half
    ins, outs = (q_in, g_in, k_in, v_in), (q_out, k_out, v_out)
    samples, tokens, _ = q_in.shape
    items = 2 * samples
    length = pairs * tokens
    span = length // BLOCKS
    mine = pl.ds(pl.multiple_of(j * tokens, tokens), tokens)
    partner = (group, 2 * j + other)

    def columns(i, pair):
        return pl.ds(pl.multiple_of((2 * pair + i % 2) * DEPTH, DEPTH), DEPTH)

    def rows_of(pair):
        return pl.ds(pl.multiple_of(pair * tokens, tokens), tokens)

    def there(i, t, side, pair):
        return pltpu.make_async_remote_copy(
            src_ref=ins[t].at[i // 2, :, columns(i, pair)], dst_ref=held.at[i, t, side, mine],
            send_sem=there_send.at[i, t, side], recv_sem=there_recv.at[i, t, side],
            device_id=(group, 2 * pair + (other if side else half)), device_id_type=MESH)

    def keep(i, t, pair):
        return pltpu.make_async_remote_copy(
            src_ref=ins[t + 2].at[i // 2, :, columns(i, pair)], dst_ref=kept.at[i, t, mine],
            send_sem=kept_send.at[i, t], recv_sem=kept_recv.at[i, t],
            device_id=(group, 2 * pair + half), device_id_type=MESH)

    def own(i, t):
        target = held.at[i, t, 0, mine] if t < 2 else kept.at[i, t - 2, mine]
        return pltpu.make_async_copy(ins[t].at[i // 2, :, columns(i, j)], target, own_sem.at[i, t])

    def back(i, o, pair):
        return pltpu.make_async_remote_copy(
            src_ref=ready.at[i, o, rows_of(pair)], dst_ref=outs[o].at[i // 2, :, columns(i, j)],
            send_sem=back_send.at[i, o], recv_sem=back_recv.at[i, o],
            device_id=(group, 2 * pair + half), device_id_type=MESH)

    def back_local(i, o):
        return pltpu.make_async_copy(ready.at[i, o, mine], outs[o].at[i // 2, :, columns(i, j)], back_own.at[i, o])

    def all_of(send, recv, count):
        rows = held.at[0, 0, 0, pl.ds(0, count * tokens)]
        return pltpu.make_async_remote_copy(
            src_ref=rows, dst_ref=rows, send_sem=send, recv_sem=recv, device_id=(group, me), device_id_type=MESH)

    def there_all(i, t, side):
        return all_of(there_send.at[i, t, side], there_recv.at[i, t, side], pairs if side else pairs - 1)

    def kept_all(i, t):
        return all_of(kept_send.at[i, t], kept_recv.at[i, t], pairs - 1)

    def back_all(i, o):
        return all_of(back_send.at[i, o], back_recv.at[i, o], pairs - 1)

    def send_back(i, o):
        back_local(i, o).start()

        @pl.loop(1, pairs)
        def _(r):
            back(i, o, lax.rem(j + r, pairs)).start()

    def send_part(i, n):
        at = pl.ds(pl.multiple_of(n * span, span), span)
        return pltpu.make_async_remote_copy(
            src_ref=part.at[i, at], dst_ref=their_part.at[i, at],
            send_sem=part_send.at[i, n], recv_sem=part_recv.at[i, n], device_id=partner, device_id_type=MESH)

    def send_stats(i):
        return pltpu.make_async_remote_copy(
            src_ref=stats.at[i], dst_ref=their_stats.at[i],
            send_sem=stats_send.at[i], recv_sem=stats_recv.at[i], device_id=partner, device_id_type=MESH)

    def issue(i):
        for t in range(2):
            @pl.loop(0, pairs)
            def _(r):
                there(i, t, 1, lax.rem(j + r, pairs)).start()

        for t in range(2):
            @pl.loop(1, pairs)
            def _(r):
                keep(i, t, lax.rem(j + r, pairs)).start()

        for t in range(2):
            @pl.loop(1, pairs)
            def _(r):
                there(i, t, 0, lax.rem(j + r, pairs)).start()

    barrier = pltpu.get_barrier_semaphore()
    seq = 2 * pairs

    @pl.loop(1, seq)
    def _(r):
        pl.semaphore_signal(barrier, inc=1, device_id=(group, lax.rem(me + r, seq)), device_id_type=MESH)

    @pl.loop(1, dps)
    def _(r):
        for side in range(2):
            pl.semaphore_signal(
                barrier, inc=1, device_id=(lax.rem(group + r, dps), 2 * j + (other if side else half)),
                device_id_type=MESH)

    for i in range(items):
        for t in range(4):
            own(i, t).start()
    gains = [
        pltpu.make_async_copy(q_gain_in, q_gain, gain_sem.at[0]),
        pltpu.make_async_copy(k_gain_in, k_gain, gain_sem.at[1]),
    ]
    for copy in gains:
        copy.start()
    pl.semaphore_wait(barrier, seq - 1 + 2 * (dps - 1))
    issue(0)
    issue(1)

    for copy in gains:
        copy.wait()
    gain_q = [q_gain[pl.ds(2 * j + e, 1)] for e in range(2)]
    gain_k = [k_gain[pl.ds(2 * j + e, 1)] for e in range(2)]
    term[...] = jnp.zeros_like(term)

    def first(i, side):
        slot, e = i % 2, i % 2

        @pl.loop(0, BLOCKS)
        def _(block):
            n, at = side * BLOCKS + block, pl.ds(pl.multiple_of(block * span, span), span)
            unit, _ = unit_of(held[i, 0, side, at])
            normed = (unit * gain_q[e]).astype(jnp.bfloat16)
            qn[slot, side, at] = normed
            top, total, dotted = weigh(
                normed, held[i, 1, side, at], kn.at[slot], kept.at[i, 1], w.at[slot, n], p.at[slot, n])
            stats[i, 0, pl.ds(n, 1)] = top
            stats[i, 1, pl.ds(n, 1)] = total
            stats[i, 2, pl.ds(n, 1)] = dotted

    def near(i):
        slot, e = i % 2, i % 2
        own(i, 2).wait()
        kept_all(i, 0).wait_recv()
        normalize(kept.at[i, 0], gain_k[e], kn.at[slot])
        knt[slot] = kn[slot].T
        own(i, 3).wait()
        kept_all(i, 1).wait_recv()
        for t in range(2):
            own(i, t).wait()
            there_all(i, t, 0).wait_recv()
        first(i, 0)

    def send_parts(i):
        @pl.loop(0, BLOCKS)
        def _(n):
            send_part(i, n).start()

    def far(i):
        for t in range(2):
            there_all(i, t, 1).wait_recv()
        if i == items - 1:
            send_parts(0)
        first(i, 1)
        send_stats(i).start()
        if i + 2 < items:
            issue(i + 2)
        if i == items - 1:
            for past in range(1, items - 2):
                send_parts(past)

    def second(i):
        slot, e = i % 2, i % 2
        send_stats(i).wait_recv()
        key_acc[...] = jnp.zeros_like(key_acc)
        value_acc[...] = jnp.zeros_like(value_acc)

        @pl.loop(0, 2 * BLOCKS)
        def _(m):
            side, block = 1 - m // BLOCKS, lax.rem(m, BLOCKS)
            n, theirs = side * BLOCKS + block, (1 - side) * BLOCKS + block
            at = pl.ds(pl.multiple_of(block * span, span), span)
            top, total, dotted = (stats[i, c, pl.ds(n, 1)] for c in range(3))
            their_top, their_total, their_dotted = (their_stats[i, c, pl.ds(theirs, 1)] for c in range(3))
            highest = jnp.maximum(top, their_top)
            here, away = jnp.exp2(top - highest), jnp.exp2(their_top - highest)
            inverse = 1.0 / (total * here + their_total * away)
            row_dot = (dotted * here + their_dotted * away) * inverse
            grad = gradients(
                qn[slot, side, at], held[i, 1, side, at], here * inverse, row_dot,
                knt.at[slot], w.at[slot, n], p.at[slot, n], key_acc, value_acc).T

            @pl.when(side == 1)
            def _():
                part[i, at] = grad.astype(jnp.bfloat16)
                if i >= items - 2:
                    send_part(i, block).start()

            @pl.when(side == 0)
            def _():
                own_part[i, at] = grad

        @pl.loop(0, BLOCKS)
        def _(n):
            at = pl.ds(pl.multiple_of(n * span, span), span)
            result, sums = norm_back(kept[i, 0, at], key_acc[at].astype(jnp.bfloat16), gain_k[e])
            ready[i, 1, at] = result
            term[e, 1:2] += sums
            ready[i, 2, at] = value_acc[at].astype(jnp.bfloat16)

        send_back(i, 1)
        send_back(i, 2)

    def last(i):
        e = i % 2

        @pl.loop(0, BLOCKS)
        def _(n):
            at = pl.ds(pl.multiple_of(n * span, span), span)
            send_part(i, n).wait_recv()
            grad = (own_part[i, at] + their_part[i, at].astype(jnp.float32)).astype(jnp.bfloat16)
            result, sums = norm_back(held[i, 0, 0, at], grad, gain_q[e])
            ready[i, 0, at] = result
            term[e, 0:1] += sums
            shift = span // tokens

            @pl.loop(0, shift)
            def _(r):
                pair = n * shift + r

                @pl.when(pair != j)
                def _():
                    back(i, 0, pair).start()

                @pl.when(pair == j)
                def _():
                    back_local(i, 0).start()

    near(0)
    far(0)
    near(1)
    far(1)
    for i in range(2, items):
        second(i - 2)
        near(i)
        far(i)
    for i in range(items - 2, items):
        second(i)
    for i in range(items):
        last(i)

    def share(r, side):
        slot = 2 * r + side
        return pltpu.make_async_remote_copy(
            src_ref=term.at[other if side else half], dst_ref=terms.at[slot],
            send_sem=term_send.at[slot], recv_sem=term_recv.at[slot],
            device_id=(lax.rem(group + r, dps), 2 * j + (other if side else half)), device_id_type=MESH)

    shares = [(r, side) for r in range(dps) for side in range(2) if r or side]
    for r, side in shares:
        share(r, side).start()
    for r, side in shares:
        share(r, side).wait()
    total = term[half]
    for r, side in shares:
        total += terms[2 * r + side]
    q_term[...] = total[0:1] * factor
    k_term[...] = total[1:2] * factor
    for i in range(items):
        send_stats(i).wait_send()
        for n in range(BLOCKS):
            send_part(i, n).wait_send()
        for t in range(2):
            kept_all(i, t).wait_send()
            for side in range(2):
                there_all(i, t, side).wait_send()
        for o in range(3):
            back_local(i, o).wait()
            back_all(i, o).wait()


def solution(mesh):
    seq, dps = mesh.shape["seq"], mesh.shape["dp"]
    pairs = seq // 2

    def step(queries, keys, values, out_grad, q_gain, k_gain):
        samples, tokens, _ = queries.shape
        items, length = 2 * samples, pairs * tokens
        assert length == BLOCKS * BQ
        vmem, anywhere = pl.BlockSpec(memory_space=pltpu.VMEM), pl.BlockSpec(memory_space=pl.ANY)
        whole = jax.ShapeDtypeStruct(queries.shape, jnp.bfloat16)
        row = jax.ShapeDtypeStruct((1, DEPTH), jnp.float32)
        dma = pltpu.SemaphoreType.DMA
        low, wide = jnp.bfloat16, jnp.float32
        return pl.pallas_call(
            functools.partial(kernel, pairs, dps, 1.0 / math.sqrt(samples * dps * seq * tokens)),
            out_shape=(whole, whole, whole, row, row),
            in_specs=[pl.BlockSpec(memory_space=pltpu.HBM)] * 6,
            out_specs=[anywhere] * 3 + [vmem] * 2,
            scratch_shapes=[
                pltpu.VMEM((items, 2, 2, length, DEPTH), low),
                pltpu.VMEM((items, 2, length, DEPTH), low),
                pltpu.VMEM((items, 3, length, DEPTH), low),
                pltpu.VMEM((2, 2, length, DEPTH), low),
                pltpu.VMEM((2, length, DEPTH), low),
                pltpu.VMEM((2, DEPTH, length), low),
                pltpu.VMEM((2, 2 * BLOCKS, length, BQ), wide),
                pltpu.VMEM((2, 2 * BLOCKS, length, BQ), wide),
                pltpu.VMEM((length, DEPTH), wide),
                pltpu.VMEM((length, DEPTH), wide),
                pltpu.VMEM((items, length, DEPTH), wide),
                pltpu.VMEM((items, length, DEPTH), low),
                pltpu.VMEM((items, length, DEPTH), low),
                pltpu.VMEM((items, 3, 2 * BLOCKS, BQ), wide),
                pltpu.VMEM((items, 3, 2 * BLOCKS, BQ), wide),
                pltpu.VMEM((2, 8, DEPTH), wide),
                pltpu.VMEM((2 * dps, 8, DEPTH), wide),
                pltpu.VMEM(q_gain.shape, wide), pltpu.VMEM(k_gain.shape, wide), dma((2,)),
                dma((items, 2, 2)), dma((items, 2, 2)), dma((items, 2)), dma((items, 2)), dma((items, 4)),
                dma((items, 3)), dma((items, 3)), dma((items, 3)),
                dma((items, BLOCKS)), dma((items, BLOCKS)), dma((items,)), dma((items,)),
                dma((2 * dps,)), dma((2 * dps,)),
            ],
            compiler_params=pltpu.CompilerParams(
                collective_id=0, has_side_effects=True, vmem_limit_bytes=60 * 2**20
            ),
        )(queries, out_grad, keys, values, q_gain, k_gain)

    return jax.shard_map(
        step,
        mesh=mesh,
        in_specs=(P("dp", "seq", None),) * 4 + (P(), P()),
        out_specs=(P("dp", "seq", None),) * 3 + (P("seq", None),) * 2,
        check_vma=False,
    )
```

```python
import functools, math
import jax, jax.numpy as jnp
from jax import lax
from jax.experimental import pallas as pl
from jax.experimental.pallas import tpu as pltpu

DEPTH = 128
SCALE = DEPTH ** -0.5
EXP_SCALE = SCALE * math.log2(math.e)
BQ = 256
CHUNK = 512
BLOCKS = 4
NT = (((1,), (1,)), ((), ()))
NN = (((1,), (0,)), ((), ()))


def dot(a, b, dims=NN):
    return lax.dot_general(a, b, dims, preferred_element_type=jnp.float32)


def unit_of(raw):
    wide = raw.astype(jnp.float32)
    rate = lax.rsqrt(jnp.mean(wide * wide, axis=-1, keepdims=True) + 1e-06)
    return wide * rate, rate


def normalize(raw_ref, gain, normed_ref, rows=256):
    @pl.loop(0, raw_ref.shape[0], step=rows)
    def _(r):
        at = pl.ds(pl.multiple_of(r, rows), rows)
        unit, _ = unit_of(raw_ref[at])
        normed_ref[at] = (unit * gain).astype(jnp.bfloat16)


def norm_back(raw, grad, gain):
    unit, rate = unit_of(raw)
    wide = grad.astype(jnp.float32)
    scaled = gain * wide
    inner = jnp.mean(scaled * unit, axis=-1, keepdims=True)
    return (rate * (scaled - unit * inner)).astype(jnp.bfloat16), jnp.sum(wide * unit, axis=0, keepdims=True)


def fold(x, op):
    rows = x.shape[0]
    out = x[:8]
    for r in range(8, rows, 8):
        out = op(out, x[r:r + 8])
    return out


from jax.sharding import PartitionSpec as P

MESH = pl.DeviceIdType.MESH


def weigh(qn, g, kn_ref, v_ref, w_ref, p_ref):
    chunks = [pl.ds(c, CHUNK) for c in range(0, kn_ref.shape[0], CHUNK)]
    top = None
    for at in chunks:
        s = dot(kn_ref[at], qn, NT)
        w_ref[at] = s
        part = fold(s, jnp.maximum)
        top = part if top is None else jnp.maximum(top, part)
    top = jnp.max(top, axis=0, keepdims=True) * EXP_SCALE
    total = dotted = None
    for at in chunks:
        w = jnp.exp2(w_ref[at] * EXP_SCALE - top)
        w_ref[at] = w
        p = dot(v_ref[at], g, NT)
        p_ref[at] = p
        a, b = fold(w, jnp.add), fold(w * p, jnp.add)
        total, dotted = (a, b) if total is None else (total + a, dotted + b)
    return top, jnp.sum(total, axis=0, keepdims=True), jnp.sum(dotted, axis=0, keepdims=True)


def gradients(qn, g, inverse, row_dot, knt_ref, w_ref, p_ref, key_acc, value_acc):
    query_t = None
    for c in range(0, w_ref.shape[0], CHUNK):
        at = pl.ds(c, CHUNK)
        probs = w_ref[at] * inverse
        value_acc[at] += dot(probs.astype(jnp.bfloat16), g)
        score_grad = (probs * (p_ref[at] - row_dot) * SCALE).astype(jnp.bfloat16)
        key_acc[at] += dot(score_grad, qn)
        part = dot(knt_ref[:, at], score_grad)
        query_t = part if query_t is None else query_t + part
    return query_t


def kernel(
    pairs, dps, factor,
    q_in, g_in, k_in, v_in, q_gain_in, k_gain_in,
    q_out, k_out, v_out, q_term, k_term,
    held, kept, ready, qn, kn, knt, w, p, key_acc, value_acc, own_part, part, their_part, tops, stats, their_stats, own_center, their_center, center_t, term, terms,
    q_gain, k_gain, gain_sem, there_send, there_recv, kept_send, kept_recv, own_sem, back_send, back_recv, back_own,
    part_send, part_recv, stats_send, stats_recv, center_send, center_recv, term_send, term_recv,
):
    me, group = lax.axis_index("seq"), lax.axis_index("dp")
    j, half = me // 2, lax.rem(me, 2)
    other = 1 - half
    ins, outs = (q_in, g_in, k_in, v_in), (q_out, k_out, v_out)
    samples, tokens, _ = q_in.shape
    items = 2 * samples
    length = pairs * tokens
    span = length // BLOCKS
    mine = pl.ds(pl.multiple_of(j * tokens, tokens), tokens)
    partner = (group, 2 * j + other)

    def columns(i, pair):
        return pl.ds(pl.multiple_of((2 * pair + i % 2) * DEPTH, DEPTH), DEPTH)

    def rows_of(pair):
        return pl.ds(pl.multiple_of(pair * tokens, tokens), tokens)

    def there(i, t, side, pair):
        return pltpu.make_async_remote_copy(
            src_ref=ins[t].at[i // 2, :, columns(i, pair)], dst_ref=held.at[i, t, side, mine],
            send_sem=there_send.at[i, t, side], recv_sem=there_recv.at[i, t, side],
            device_id=(group, 2 * pair + (other if side else half)), device_id_type=MESH)

    def keep(i, t, pair):
        return pltpu.make_async_remote_copy(
            src_ref=ins[t + 2].at[i // 2, :, columns(i, pair)], dst_ref=kept.at[i, t, mine],
            send_sem=kept_send.at[i, t], recv_sem=kept_recv.at[i, t],
            device_id=(group, 2 * pair + half), device_id_type=MESH)

    def own(i, t):
        target = held.at[i, t, 0, mine] if t < 2 else kept.at[i, t - 2, mine]
        return pltpu.make_async_copy(ins[t].at[i // 2, :, columns(i, j)], target, own_sem.at[i, t])

    def back(i, o, pair):
        return pltpu.make_async_remote_copy(
            src_ref=ready.at[i, o, rows_of(pair)], dst_ref=outs[o].at[i // 2, :, columns(i, j)],
            send_sem=back_send.at[i, o], recv_sem=back_recv.at[i, o],
            device_id=(group, 2 * pair + half), device_id_type=MESH)

    def back_local(i, o):
        return pltpu.make_async_copy(ready.at[i, o, mine], outs[o].at[i // 2, :, columns(i, j)], back_own.at[i, o])

    def all_of(send, recv, count):
        rows = held.at[0, 0, 0, pl.ds(0, count * tokens)]
        return pltpu.make_async_remote_copy(
            src_ref=rows, dst_ref=rows, send_sem=send, recv_sem=recv, device_id=(group, me), device_id_type=MESH)

    def there_all(i, t, side):
        return all_of(there_send.at[i, t, side], there_recv.at[i, t, side], pairs if side else pairs - 1)

    def kept_all(i, t):
        return all_of(kept_send.at[i, t], kept_recv.at[i, t], pairs - 1)

    def back_all(i, o):
        return all_of(back_send.at[i, o], back_recv.at[i, o], pairs - 1)

    def send_back(i, o):
        back_local(i, o).start()

        @pl.loop(1, pairs)
        def _(r):
            back(i, o, lax.rem(j + r, pairs)).start()

    def send_part(i, n):
        at = pl.ds(pl.multiple_of(n * span, span), span)
        return pltpu.make_async_remote_copy(
            src_ref=part.at[i, at], dst_ref=their_part.at[i, at],
            send_sem=part_send.at[i, n], recv_sem=part_recv.at[i, n], device_id=partner, device_id_type=MESH)

    def send_stats(i):
        return pltpu.make_async_remote_copy(
            src_ref=stats.at[i], dst_ref=their_stats.at[i],
            send_sem=stats_send.at[i], recv_sem=stats_recv.at[i], device_id=partner, device_id_type=MESH)

    def send_center(i):
        return pltpu.make_async_remote_copy(
            src_ref=own_center.at[i], dst_ref=their_center.at[i],
            send_sem=center_send.at[i], recv_sem=center_recv.at[i], device_id=partner, device_id_type=MESH)

    def issue(i):
        for t in range(2):
            @pl.loop(0, pairs)
            def _(r):
                there(i, t, 1, lax.rem(j + r, pairs)).start()

        for t in range(2):
            @pl.loop(1, pairs)
            def _(r):
                keep(i, t, lax.rem(j + r, pairs)).start()

        for t in range(2):
            @pl.loop(1, pairs)
            def _(r):
                there(i, t, 0, lax.rem(j + r, pairs)).start()

    barrier = pltpu.get_barrier_semaphore()
    seq = 2 * pairs

    @pl.loop(1, seq)
    def _(r):
        pl.semaphore_signal(barrier, inc=1, device_id=(group, lax.rem(me + r, seq)), device_id_type=MESH)

    @pl.loop(1, dps)
    def _(r):
        for side in range(2):
            pl.semaphore_signal(
                barrier, inc=1, device_id=(lax.rem(group + r, dps), 2 * j + (other if side else half)),
                device_id_type=MESH)

    for i in range(items):
        for t in range(4):
            own(i, t).start()
    gains = [
        pltpu.make_async_copy(q_gain_in, q_gain, gain_sem.at[0]),
        pltpu.make_async_copy(k_gain_in, k_gain, gain_sem.at[1]),
    ]
    for copy in gains:
        copy.start()
    pl.semaphore_wait(barrier, seq - 1 + 2 * (dps - 1))
    issue(0)
    issue(1)

    for copy in gains:
        copy.wait()
    gain_q = [q_gain[pl.ds(2 * j + e, 1)] for e in range(2)]
    gain_k = [k_gain[pl.ds(2 * j + e, 1)] for e in range(2)]
    term[...] = jnp.zeros_like(term)

    def first(i, side):
        slot, e = i % 2, i % 2

        @pl.loop(0, BLOCKS)
        def _(block):
            n, at = side * BLOCKS + block, pl.ds(pl.multiple_of(block * span, span), span)
            unit, _ = unit_of(held[i, 0, side, at])
            normed = (unit * gain_q[e]).astype(jnp.bfloat16)
            qn[slot, side, at] = normed
            top, total, dotted = weigh(
                normed, held[i, 1, side, at], kn.at[slot], kept.at[i, 1], w.at[slot, n], p.at[slot, n])
            tops[slot, pl.ds(n, 1)] = top
            stats[i, 0, pl.ds(n, 1)] = top + jnp.log2(total)
            stats[i, 1, pl.ds(n, 1)] = dotted / total

    def near(i):
        slot, e = i % 2, i % 2
        own(i, 2).wait()
        kept_all(i, 0).wait_recv()
        normalize(kept.at[i, 0], gain_k[e], kn.at[slot])
        knt[slot] = kn[slot].T
        mean = jnp.mean(kn[slot].astype(jnp.float32), axis=0, keepdims=True)
        own_center[i] = jnp.broadcast_to(mean, (8, DEPTH))
        send_center(i).start()
        own(i, 3).wait()
        kept_all(i, 1).wait_recv()
        for t in range(2):
            own(i, t).wait()
            there_all(i, t, 0).wait_recv()
        first(i, 0)

    def send_parts(i):
        @pl.loop(0, BLOCKS)
        def _(n):
            send_part(i, n).start()

    def far(i):
        for t in range(2):
            there_all(i, t, 1).wait_recv()
        if i == items - 1:
            send_parts(0)
        first(i, 1)
        send_stats(i).start()
        if i + 2 < items:
            issue(i + 2)
        if i == items - 1:
            for past in range(1, items - 2):
                send_parts(past)

    def second(i):
        slot, e = i % 2, i % 2
        send_stats(i).wait_recv()
        send_center(i).wait_recv()
        for side, center in enumerate((their_center, own_center)):
            center_t[side] = jnp.broadcast_to(center[i, 0:1], (BQ, DEPTH)).T
        key_acc[...] = jnp.zeros_like(key_acc)
        value_acc[...] = jnp.zeros_like(value_acc)

        @pl.loop(0, 2 * BLOCKS)
        def _(m):
            side, block = 1 - m // BLOCKS, lax.rem(m, BLOCKS)
            n, theirs = side * BLOCKS + block, (1 - side) * BLOCKS + block
            at = pl.ds(pl.multiple_of(block * span, span), span)
            level, dotted = (stats[i, c, pl.ds(n, 1)] for c in range(2))
            their_level, their_dotted = (their_stats[i, c, pl.ds(theirs, 1)] for c in range(2))
            highest = jnp.maximum(level, their_level)
            here, away = jnp.exp2(level - highest), jnp.exp2(their_level - highest)
            inverse = 1.0 / (here + away)
            row_dot = (dotted * here + their_dotted * away) * inverse
            scale = jnp.exp2(tops[slot, pl.ds(n, 1)] - highest) * inverse
            gone = here * inverse * (row_dot - dotted) * SCALE
            back_in = away * inverse * (their_dotted - row_dot) * SCALE
            grad = gradients(
                qn[slot, side, at], held[i, 1, side, at], scale, row_dot,
                knt.at[slot], w.at[slot, n], p.at[slot, n], key_acc, value_acc)
            grad = (grad + center_t[side] * jnp.where(side == 1, gone, back_in)).T
            unit, _ = unit_of(held[i, 0, side, at])
            term[e, 0:1] += jnp.sum(grad * unit, axis=0, keepdims=True)

            @pl.when(side == 1)
            def _():
                part[i, at] = grad.astype(jnp.bfloat16)
                if i >= items - 2:
                    send_part(i, block).start()

            @pl.when(side == 0)
            def _():
                own_part[i, at] = grad

        @pl.loop(0, BLOCKS)
        def _(n):
            at = pl.ds(pl.multiple_of(n * span, span), span)
            result, sums = norm_back(kept[i, 0, at], key_acc[at].astype(jnp.bfloat16), gain_k[e])
            ready[i, 1, at] = result
            term[e, 1:2] += sums
            ready[i, 2, at] = value_acc[at].astype(jnp.bfloat16)

        send_back(i, 1)
        send_back(i, 2)

    def last(i):
        e = i % 2

        @pl.loop(0, BLOCKS)
        def _(n):
            at = pl.ds(pl.multiple_of(n * span, span), span)
            send_part(i, n).wait_recv()
            grad = (own_part[i, at] + their_part[i, at].astype(jnp.float32)).astype(jnp.bfloat16)
            ready[i, 0, at], _ = norm_back(held[i, 0, 0, at], grad, gain_q[e])
            shift = span // tokens

            @pl.loop(0, shift)
            def _(r):
                pair = n * shift + r

                @pl.when(pair != j)
                def _():
                    back(i, 0, pair).start()

                @pl.when(pair == j)
                def _():
                    back_local(i, 0).start()

    near(0)
    far(0)
    near(1)
    far(1)
    for i in range(2, items):
        second(i - 2)
        near(i)
        far(i)
    for i in range(items - 2, items):
        second(i)
    def share(r, side):
        slot = 2 * r + side
        return pltpu.make_async_remote_copy(
            src_ref=term.at[other if side else half], dst_ref=terms.at[slot],
            send_sem=term_send.at[slot], recv_sem=term_recv.at[slot],
            device_id=(lax.rem(group + r, dps), 2 * j + (other if side else half)), device_id_type=MESH)

    shares = [(r, side) for r in range(dps) for side in range(2) if r or side]
    for r, side in shares:
        share(r, side).start()
    for i in range(items):
        last(i)
    for r, side in shares:
        share(r, side).wait()
    total = term[half]
    for r, side in shares:
        total += terms[2 * r + side]
    q_term[...] = total[0:1] * factor
    k_term[...] = total[1:2] * factor
    for i in range(items):
        send_stats(i).wait_send()
        send_center(i).wait_send()
        for n in range(BLOCKS):
            send_part(i, n).wait_send()
        for t in range(2):
            kept_all(i, t).wait_send()
            for side in range(2):
                there_all(i, t, side).wait_send()
        for o in range(3):
            back_local(i, o).wait()
            back_all(i, o).wait()


def hand_over(*refs):
    sems = refs[-1]
    copies = [pltpu.make_async_copy(src, dst, sems.at[c]) for c, (src, dst) in enumerate(zip(refs[:5], refs[5:10]))]
    for copy in copies:
        copy.start()
    for copy in copies:
        copy.wait()


def solution(mesh):
    seq, dps = mesh.shape["seq"], mesh.shape["dp"]
    pairs = seq // 2

    def step(queries, keys, values, out_grad, q_gain, k_gain):
        samples, tokens, _ = queries.shape
        items, length = 2 * samples, pairs * tokens
        assert length == BLOCKS * BQ
        vmem = pl.BlockSpec(memory_space=pltpu.VMEM)
        whole = jax.ShapeDtypeStruct(queries.shape, jnp.bfloat16)
        row = jax.ShapeDtypeStruct((1, DEPTH), jnp.float32)
        dma = pltpu.SemaphoreType.DMA
        low, wide = jnp.bfloat16, jnp.float32
        results = pl.pallas_call(
            functools.partial(kernel, pairs, dps, 1.0 / math.sqrt(samples * dps * seq * tokens)),
            out_shape=(pltpu.VMEM(whole.shape, low),) * 3 + (pltpu.VMEM(row.shape, wide),) * 2,
            in_specs=[pl.BlockSpec(memory_space=pltpu.HBM)] * 6,
            out_specs=[vmem] * 5,
            scratch_shapes=[
                pltpu.VMEM((items, 2, 2, length, DEPTH), low),
                pltpu.VMEM((items, 2, length, DEPTH), low),
                pltpu.VMEM((items, 3, length, DEPTH), low),
                pltpu.VMEM((2, 2, length, DEPTH), low),
                pltpu.VMEM((2, length, DEPTH), low),
                pltpu.VMEM((2, DEPTH, length), low),
                pltpu.VMEM((2, 2 * BLOCKS, length, BQ), wide),
                pltpu.VMEM((2, 2 * BLOCKS, length, BQ), wide),
                pltpu.VMEM((length, DEPTH), wide),
                pltpu.VMEM((length, DEPTH), wide),
                pltpu.VMEM((items, length, DEPTH), wide),
                pltpu.VMEM((items, length, DEPTH), low),
                pltpu.VMEM((items, length, DEPTH), low),
                pltpu.VMEM((2, 2 * BLOCKS, BQ), wide),
                pltpu.VMEM((items, 2, 2 * BLOCKS, BQ), wide),
                pltpu.VMEM((items, 2, 2 * BLOCKS, BQ), wide),
                pltpu.VMEM((items, 8, DEPTH), wide),
                pltpu.VMEM((items, 8, DEPTH), wide),
                pltpu.VMEM((2, DEPTH, BQ), wide),
                pltpu.VMEM((2, 8, DEPTH), wide),
                pltpu.VMEM((2 * dps, 8, DEPTH), wide),
                pltpu.VMEM(q_gain.shape, wide), pltpu.VMEM(k_gain.shape, wide), dma((2,)),
                dma((items, 2, 2)), dma((items, 2, 2)), dma((items, 2)), dma((items, 2)), dma((items, 4)),
                dma((items, 3)), dma((items, 3)), dma((items, 3)),
                dma((items, BLOCKS)), dma((items, BLOCKS)), dma((items,)), dma((items,)), dma((items,)), dma((items,)),
                dma((2 * dps,)), dma((2 * dps,)),
            ],
            compiler_params=pltpu.CompilerParams(
                collective_id=0, has_side_effects=True, vmem_limit_bytes=52 * 2**20
            ),
        )(queries, out_grad, keys, values, q_gain, k_gain)
        hbm = pl.BlockSpec(memory_space=pltpu.HBM)
        return pl.pallas_call(
            hand_over,
            out_shape=(pltpu.HBM(whole.shape, low),) * 3 + (pltpu.HBM(row.shape, wide),) * 2,
            in_specs=[vmem] * 5,
            out_specs=[hbm] * 5,
            scratch_shapes=[dma((5,))],
        )(*(pltpu.with_memory_space_constraint(x, pltpu.VMEM) for x in results))

    return jax.shard_map(
        step,
        mesh=mesh,
        in_specs=(P("dp", "seq", None),) * 4 + (P(), P()),
        out_specs=(P("dp", "seq", None),) * 3 + (P("seq", None),) * 2,
        check_vma=False,
    )
```

```python
import functools, math
import jax, jax.numpy as jnp
from jax import lax
from jax.experimental import pallas as pl
from jax.experimental.pallas import tpu as pltpu

DEPTH = 128
SCALE = DEPTH ** -0.5
EXP_SCALE = SCALE * math.log2(math.e)
BQ = 256
CHUNK = 512
BLOCKS = 4
NT = (((1,), (1,)), ((), ()))
NN = (((1,), (0,)), ((), ()))


def dot(a, b, dims=NN):
    return lax.dot_general(a, b, dims, preferred_element_type=jnp.float32)


def unit_of(raw):
    wide = raw.astype(jnp.float32)
    rate = lax.rsqrt(jnp.mean(wide * wide, axis=-1, keepdims=True) + 1e-06)
    return wide * rate, rate


def normalize(raw_ref, gain, normed_ref, rows=256):
    @pl.loop(0, raw_ref.shape[0], step=rows)
    def _(r):
        at = pl.ds(pl.multiple_of(r, rows), rows)
        unit, _ = unit_of(raw_ref[at])
        normed_ref[at] = (unit * gain).astype(jnp.bfloat16)


def norm_back(raw, grad, gain):
    unit, rate = unit_of(raw)
    wide = grad.astype(jnp.float32)
    scaled = gain * wide
    inner = jnp.mean(scaled * unit, axis=-1, keepdims=True)
    return (rate * (scaled - unit * inner)).astype(jnp.bfloat16), jnp.sum(wide * unit, axis=0, keepdims=True)


def fold(x, op):
    rows = x.shape[0]
    out = x[:8]
    for r in range(8, rows, 8):
        out = op(out, x[r:r + 8])
    return out


from jax.sharding import PartitionSpec as P

MESH = pl.DeviceIdType.MESH


def weigh(qn, g, kn_ref, v_ref, w_ref, p_ref):
    chunks = [pl.ds(c, CHUNK) for c in range(0, kn_ref.shape[0], CHUNK)]
    top = None
    for at in chunks:
        s = dot(kn_ref[at], qn, NT)
        w_ref[at] = s
        part = fold(s, jnp.maximum)
        top = part if top is None else jnp.maximum(top, part)
    top = jnp.max(top, axis=0, keepdims=True) * EXP_SCALE
    total = dotted = None
    for at in chunks:
        w = jnp.exp2(w_ref[at] * EXP_SCALE - top)
        w_ref[at] = w
        p = dot(v_ref[at], g, NT)
        p_ref[at] = p
        a, b = fold(w, jnp.add), fold(w * p, jnp.add)
        total, dotted = (a, b) if total is None else (total + a, dotted + b)
    return top, jnp.sum(total, axis=0, keepdims=True), jnp.sum(dotted, axis=0, keepdims=True)


def gradients(qn, g, inverse, row_dot, knt_ref, w_ref, p_ref, key_acc, value_acc):
    query_t = None
    for c in range(0, w_ref.shape[0], CHUNK):
        at = pl.ds(c, CHUNK)
        probs = w_ref[at] * inverse
        value_acc[at] += dot(probs.astype(jnp.bfloat16), g)
        score_grad = (probs * (p_ref[at] - row_dot) * SCALE).astype(jnp.bfloat16)
        key_acc[at] += dot(score_grad, qn)
        part = dot(knt_ref[:, at], score_grad)
        query_t = part if query_t is None else query_t + part
    return query_t


def kernel(
    pairs, dps, factor,
    q_in, g_in, k_in, v_in, q_gain_in, k_gain_in,
    q_out, k_out, v_out, q_term, k_term,
    held, kept, ready, units, qn, kn, knt, w, p, key_acc, value_acc, own_part, part, their_part, tops, stats, their_stats, own_center, their_center, center_t, term, terms,
    q_gain, k_gain, gain_sem, there_send, there_recv, kept_send, kept_recv, own_sem, back_send, back_recv, back_own,
    part_send, part_recv, stats_send, stats_recv, center_send, center_recv, term_send, term_recv,
):
    me, group = lax.axis_index("seq"), lax.axis_index("dp")
    j, half = me // 2, lax.rem(me, 2)
    other = 1 - half
    turn = j // (pairs // BLOCKS)
    ins, outs = (q_in, g_in, k_in, v_in), (q_out, k_out, v_out)
    samples, tokens, _ = q_in.shape
    items = 2 * samples
    length = pairs * tokens
    span = length // BLOCKS
    mine = pl.ds(pl.multiple_of(j * tokens, tokens), tokens)
    partner = (group, 2 * j + other)

    def columns(i, pair):
        return pl.ds(pl.multiple_of((2 * pair + i % 2) * DEPTH, DEPTH), DEPTH)

    def rows_of(pair):
        return pl.ds(pl.multiple_of(pair * tokens, tokens), tokens)

    def there(i, t, side, pair):
        return pltpu.make_async_remote_copy(
            src_ref=ins[t].at[i // 2, :, columns(i, pair)], dst_ref=held.at[i, t, side, mine],
            send_sem=there_send.at[i, t, side], recv_sem=there_recv.at[i, t, side],
            device_id=(group, 2 * pair + (other if side else half)), device_id_type=MESH)

    def keep(i, t, pair):
        return pltpu.make_async_remote_copy(
            src_ref=ins[t + 2].at[i // 2, :, columns(i, pair)], dst_ref=kept.at[i, t, mine],
            send_sem=kept_send.at[i, t], recv_sem=kept_recv.at[i, t],
            device_id=(group, 2 * pair + half), device_id_type=MESH)

    def own(i, t):
        target = held.at[i, t, 0, mine] if t < 2 else kept.at[i, t - 2, mine]
        return pltpu.make_async_copy(ins[t].at[i // 2, :, columns(i, j)], target, own_sem.at[i, t])

    def back(i, o, pair):
        return pltpu.make_async_remote_copy(
            src_ref=ready.at[i, o, rows_of(pair)], dst_ref=outs[o].at[i // 2, :, columns(i, j)],
            send_sem=back_send.at[i, o], recv_sem=back_recv.at[i, o],
            device_id=(group, 2 * pair + half), device_id_type=MESH)

    def back_local(i, o):
        return pltpu.make_async_copy(ready.at[i, o, mine], outs[o].at[i // 2, :, columns(i, j)], back_own.at[i, o])

    def all_of(send, recv, count):
        rows = held.at[0, 0, 0, pl.ds(0, count * tokens)]
        return pltpu.make_async_remote_copy(
            src_ref=rows, dst_ref=rows, send_sem=send, recv_sem=recv, device_id=(group, me), device_id_type=MESH)

    def there_all(i, t, side):
        return all_of(there_send.at[i, t, side], there_recv.at[i, t, side], pairs if side else pairs - 1)

    def kept_all(i, t):
        return all_of(kept_send.at[i, t], kept_recv.at[i, t], pairs - 1)

    def back_all(i, o):
        return all_of(back_send.at[i, o], back_recv.at[i, o], pairs - 1)

    def send_back(i, o):
        back_local(i, o).start()

        @pl.loop(1, pairs)
        def _(r):
            back(i, o, lax.rem(j + r, pairs)).start()

    def send_part(i, n):
        at = pl.ds(pl.multiple_of(n * span, span), span)
        return pltpu.make_async_remote_copy(
            src_ref=part.at[i, at], dst_ref=their_part.at[i, at],
            send_sem=part_send.at[i, n], recv_sem=part_recv.at[i, n], device_id=partner, device_id_type=MESH)

    def send_stats(i):
        return pltpu.make_async_remote_copy(
            src_ref=stats.at[i], dst_ref=their_stats.at[i],
            send_sem=stats_send.at[i], recv_sem=stats_recv.at[i], device_id=partner, device_id_type=MESH)

    def send_center(i):
        return pltpu.make_async_remote_copy(
            src_ref=own_center.at[i], dst_ref=their_center.at[i],
            send_sem=center_send.at[i], recv_sem=center_recv.at[i], device_id=partner, device_id_type=MESH)

    def issue(i):
        for t in range(2):
            @pl.loop(0, pairs)
            def _(r):
                there(i, t, 1, lax.rem(j + r, pairs)).start()

        for t in range(2):
            @pl.loop(1, pairs)
            def _(r):
                keep(i, t, lax.rem(j + r, pairs)).start()

        for t in range(2):
            @pl.loop(1, pairs)
            def _(r):
                there(i, t, 0, lax.rem(j + r, pairs)).start()

    barrier = pltpu.get_barrier_semaphore()
    seq = 2 * pairs

    @pl.loop(1, seq)
    def _(r):
        pl.semaphore_signal(barrier, inc=1, device_id=(group, lax.rem(me + r, seq)), device_id_type=MESH)

    @pl.loop(1, dps)
    def _(r):
        for side in range(2):
            pl.semaphore_signal(
                barrier, inc=1, device_id=(lax.rem(group + r, dps), 2 * j + (other if side else half)),
                device_id_type=MESH)

    for i in range(items):
        for t in range(4):
            own(i, t).start()
    gains = [
        pltpu.make_async_copy(q_gain_in, q_gain, gain_sem.at[0]),
        pltpu.make_async_copy(k_gain_in, k_gain, gain_sem.at[1]),
    ]
    for copy in gains:
        copy.start()
    pl.semaphore_wait(barrier, seq - 1 + 2 * (dps - 1))
    issue(0)
    issue(1)
    issue(2)

    for copy in gains:
        copy.wait()
    gain_q = [q_gain[pl.ds(2 * j + e, 1)] for e in range(2)]
    gain_k = [k_gain[pl.ds(2 * j + e, 1)] for e in range(2)]
    term[...] = jnp.zeros_like(term)

    def first(i, side):
        slot, e = i % 2, i % 2

        @pl.loop(0, BLOCKS)
        def _(block):
            n, at = side * BLOCKS + block, pl.ds(pl.multiple_of(block * span, span), span)
            unit, _ = unit_of(held[i, 0, side, at])
            units[slot, side, at] = unit
            normed = (unit * gain_q[e]).astype(jnp.bfloat16)
            qn[slot, side, at] = normed
            top, total, dotted = weigh(
                normed, held[i, 1, side, at], kn.at[slot], kept.at[i, 1], w.at[slot, n], p.at[slot, n])
            tops[slot, pl.ds(n, 1)] = top
            stats[i, 0, pl.ds(n, 1)] = top + jnp.log2(total)
            stats[i, 1, pl.ds(n, 1)] = dotted / total

    def near(i):
        slot, e = i % 2, i % 2
        own(i, 2).wait()
        kept_all(i, 0).wait_recv()
        normalize(kept.at[i, 0], gain_k[e], kn.at[slot])
        knt[slot] = kn[slot].T
        mean = jnp.mean(kn[slot].astype(jnp.float32), axis=0, keepdims=True)
        own_center[i] = mean
        send_center(i).start()
        own(i, 3).wait()
        kept_all(i, 1).wait_recv()
        for t in range(2):
            own(i, t).wait()
            there_all(i, t, 0).wait_recv()
        first(i, 0)

    def send_parts(i):
        @pl.loop(0, BLOCKS)
        def _(n):
            send_part(i, lax.rem(n + turn, BLOCKS)).start()

    def far(i):
        for t in range(2):
            there_all(i, t, 1).wait_recv()
        first(i, 1)
        send_stats(i).start()
        if i + 3 < items:
            issue(i + 3)
        if i == items - 1:
            for past in range(1, items - 2):
                send_parts(past)

    def second(i):
        slot, e = i % 2, i % 2
        send_stats(i).wait_recv()
        send_center(i).wait_recv()
        for side, center in enumerate((their_center, own_center)):
            center_t[side] = jnp.broadcast_to(center[i], (BQ, DEPTH)).T
        key_acc[...] = jnp.zeros_like(key_acc)
        value_acc[...] = jnp.zeros_like(value_acc)

        @pl.loop(0, 2 * BLOCKS)
        def _(m):
            side, block = 1 - m // BLOCKS, lax.rem(m + turn, BLOCKS)
            n, theirs = side * BLOCKS + block, (1 - side) * BLOCKS + block
            at = pl.ds(pl.multiple_of(block * span, span), span)
            level, dotted = (stats[i, c, pl.ds(n, 1)] for c in range(2))
            their_level, their_dotted = (their_stats[i, c, pl.ds(theirs, 1)] for c in range(2))
            highest = jnp.maximum(level, their_level)
            here, away = jnp.exp2(level - highest), jnp.exp2(their_level - highest)
            inverse = 1.0 / (here + away)
            row_dot = (dotted * here + their_dotted * away) * inverse
            scale = jnp.exp2(tops[slot, pl.ds(n, 1)] - highest) * inverse
            gone = here * inverse * (row_dot - dotted) * SCALE
            back_in = away * inverse * (their_dotted - row_dot) * SCALE
            grad = gradients(
                qn[slot, side, at], held[i, 1, side, at], scale, row_dot,
                knt.at[slot], w.at[slot, n], p.at[slot, n], key_acc, value_acc)
            grad = (grad + center_t[side] * jnp.where(side == 1, gone, back_in)).T
            term[e, 0:1] += jnp.sum(grad * units[slot, side, at], axis=0, keepdims=True)

            @pl.when(side == 1)
            def _():
                part[i, at] = grad.astype(jnp.bfloat16)
                if i != 1:
                    send_part(i, block).start()

            @pl.when(side == 0)
            def _():
                own_part[i, at] = grad

        @pl.loop(0, BLOCKS)
        def _(n):
            at = pl.ds(pl.multiple_of(n * span, span), span)
            result, sums = norm_back(kept[i, 0, at], key_acc[at].astype(jnp.bfloat16), gain_k[e])
            ready[i, 1, at] = result
            term[e, 1:2] += sums
            ready[i, 2, at] = value_acc[at].astype(jnp.bfloat16)

        send_back(i, 1)
        send_back(i, 2)

    def last(i):
        e = i % 2

        @pl.loop(0, BLOCKS)
        def _(m):
            n = lax.rem(m + turn, BLOCKS)
            at = pl.ds(pl.multiple_of(n * span, span), span)
            send_part(i, n).wait_recv()
            grad = (own_part[i, at] + their_part[i, at].astype(jnp.float32)).astype(jnp.bfloat16)
            ready[i, 0, at], _ = norm_back(held[i, 0, 0, at], grad, gain_q[e])
            shift = span // tokens

            @pl.loop(0, shift)
            def _(r):
                pair = n * shift + r

                @pl.when(pair != j)
                def _():
                    back(i, 0, pair).start()

                @pl.when(pair == j)
                def _():
                    back_local(i, 0).start()

    near(0)
    far(0)
    near(1)
    far(1)
    for i in range(2, items):
        second(i - 2)
        near(i)
        far(i)
    second(items - 2)
    last(0)
    second(items - 1)
    def share(r, side):
        slot = 2 * r + side
        return pltpu.make_async_remote_copy(
            src_ref=term.at[other if side else half], dst_ref=terms.at[slot],
            send_sem=term_send.at[slot], recv_sem=term_recv.at[slot],
            device_id=(lax.rem(group + r, dps), 2 * j + (other if side else half)), device_id_type=MESH)

    shares = [(r, side) for r in range(dps) for side in range(2) if r or side]
    for r, side in shares:
        share(r, side).start()
    for i in range(1, items):
        last(i)
    for r, side in shares:
        share(r, side).wait()
    total = term[half]
    for r, side in shares:
        total += terms[2 * r + side]
    q_term[...] = total[0:1] * factor
    k_term[...] = total[1:2] * factor
    for i in range(items):
        send_stats(i).wait_send()
        send_center(i).wait_send()
        for n in range(BLOCKS):
            send_part(i, n).wait_send()
        for t in range(2):
            kept_all(i, t).wait_send()
            for side in range(2):
                there_all(i, t, side).wait_send()
        for o in range(3):
            back_local(i, o).wait()
            back_all(i, o).wait()


def hand_over(*refs):
    sems = refs[-1]
    copies = [pltpu.make_async_copy(src, dst, sems.at[c]) for c, (src, dst) in enumerate(zip(refs[:5], refs[5:10]))]
    for copy in copies:
        copy.start()
    for copy in copies:
        copy.wait()


def solution(mesh):
    seq, dps = mesh.shape["seq"], mesh.shape["dp"]
    pairs = seq // 2

    def step(queries, keys, values, out_grad, q_gain, k_gain):
        samples, tokens, _ = queries.shape
        items, length = 2 * samples, pairs * tokens
        assert length == BLOCKS * BQ
        vmem = pl.BlockSpec(memory_space=pltpu.VMEM)
        whole = jax.ShapeDtypeStruct(queries.shape, jnp.bfloat16)
        row = jax.ShapeDtypeStruct((1, DEPTH), jnp.float32)
        dma = pltpu.SemaphoreType.DMA
        low, wide = jnp.bfloat16, jnp.float32
        results = pl.pallas_call(
            functools.partial(kernel, pairs, dps, 1.0 / math.sqrt(samples * dps * seq * tokens)),
            out_shape=(pltpu.VMEM(whole.shape, low),) * 3 + (pltpu.VMEM(row.shape, wide),) * 2,
            in_specs=[pl.BlockSpec(memory_space=pltpu.HBM)] * 6,
            out_specs=[vmem] * 5,
            scratch_shapes=[
                pltpu.VMEM((items, 2, 2, length, DEPTH), low),
                pltpu.VMEM((items, 2, length, DEPTH), low),
                pltpu.VMEM((items, 3, length, DEPTH), low),
                pltpu.VMEM((2, 2, length, DEPTH), wide),
                pltpu.VMEM((2, 2, length, DEPTH), low),
                pltpu.VMEM((2, length, DEPTH), low),
                pltpu.VMEM((2, DEPTH, length), low),
                pltpu.VMEM((2, 2 * BLOCKS, length, BQ), wide),
                pltpu.VMEM((2, 2 * BLOCKS, length, BQ), wide),
                pltpu.VMEM((length, DEPTH), wide),
                pltpu.VMEM((length, DEPTH), wide),
                pltpu.VMEM((items, length, DEPTH), wide),
                pltpu.VMEM((items, length, DEPTH), low),
                pltpu.VMEM((items, length, DEPTH), low),
                pltpu.VMEM((2, 2 * BLOCKS, BQ), wide),
                pltpu.VMEM((items, 2, 2 * BLOCKS, BQ), wide),
                pltpu.VMEM((items, 2, 2 * BLOCKS, BQ), wide),
                pltpu.VMEM((items, 1, DEPTH), wide),
                pltpu.VMEM((items, 1, DEPTH), wide),
                pltpu.VMEM((2, DEPTH, BQ), wide),
                pltpu.VMEM((2, 2, DEPTH), wide),
                pltpu.VMEM((2 * dps, 2, DEPTH), wide),
                pltpu.VMEM(q_gain.shape, wide), pltpu.VMEM(k_gain.shape, wide), dma((2,)),
                dma((items, 2, 2)), dma((items, 2, 2)), dma((items, 2)), dma((items, 2)), dma((items, 4)),
                dma((items, 3)), dma((items, 3)), dma((items, 3)),
                dma((items, BLOCKS)), dma((items, BLOCKS)), dma((items,)), dma((items,)), dma((items,)), dma((items,)),
                dma((2 * dps,)), dma((2 * dps,)),
            ],
            compiler_params=pltpu.CompilerParams(
                collective_id=0, has_side_effects=True, vmem_limit_bytes=54 * 2**20
            ),
        )(queries, out_grad, keys, values, q_gain, k_gain)
        hbm = pl.BlockSpec(memory_space=pltpu.HBM)
        return pl.pallas_call(
            hand_over,
            out_shape=(pltpu.HBM(whole.shape, low),) * 3 + (pltpu.HBM(row.shape, wide),) * 2,
            in_specs=[vmem] * 5,
            out_specs=[hbm] * 5,
            scratch_shapes=[dma((5,))],
        )(*(pltpu.with_memory_space_constraint(x, pltpu.VMEM) for x in results))

    return jax.shard_map(
        step,
        mesh=mesh,
        in_specs=(P("dp", "seq", None),) * 4 + (P(), P()),
        out_specs=(P("dp", "seq", None),) * 3 + (P("seq", None),) * 2,
        check_vma=False,
    )
```

```python
import functools, math
import jax, jax.numpy as jnp
from jax import lax
from jax.experimental import pallas as pl
from jax.experimental.pallas import tpu as pltpu

DEPTH = 128
SCALE = DEPTH ** -0.5
EXP_SCALE = SCALE * math.log2(math.e)
BQ = 256
CHUNK = 512
BLOCKS = 4
NT = (((1,), (1,)), ((), ()))
NN = (((1,), (0,)), ((), ()))


def dot(a, b, dims=NN):
    return lax.dot_general(a, b, dims, preferred_element_type=jnp.float32)


def unit_of(raw):
    wide = raw.astype(jnp.float32)
    rate = lax.rsqrt(jnp.mean(wide * wide, axis=-1, keepdims=True) + 1e-06)
    return wide * rate, rate


def normalize(raw_ref, gain, normed_ref, rows=256):
    @pl.loop(0, raw_ref.shape[0], step=rows)
    def _(r):
        at = pl.ds(pl.multiple_of(r, rows), rows)
        unit, _ = unit_of(raw_ref[at])
        normed_ref[at] = (unit * gain).astype(jnp.bfloat16)


def norm_back(raw, grad, gain):
    unit, rate = unit_of(raw)
    wide = grad.astype(jnp.float32)
    scaled = gain * wide
    inner = jnp.mean(scaled * unit, axis=-1, keepdims=True)
    return (rate * (scaled - unit * inner)).astype(jnp.bfloat16), jnp.sum(wide * unit, axis=0, keepdims=True)


def fold(x, op):
    rows = x.shape[0]
    out = x[:8]
    for r in range(8, rows, 8):
        out = op(out, x[r:r + 8])
    return out


from jax.sharding import PartitionSpec as P

MESH = pl.DeviceIdType.MESH


def weigh(qn, g, kn_ref, v_ref, w_ref, p_ref):
    chunks = [pl.ds(c, CHUNK) for c in range(0, kn_ref.shape[0], CHUNK)]
    top = None
    for at in chunks:
        s = dot(kn_ref[at], qn, NT)
        w_ref[at] = s
        part = fold(s, jnp.maximum)
        top = part if top is None else jnp.maximum(top, part)
    top = jnp.max(top, axis=0, keepdims=True) * EXP_SCALE
    total = dotted = None
    for at in chunks:
        w = jnp.exp2(w_ref[at] * EXP_SCALE - top)
        w_ref[at] = w
        p = dot(v_ref[at], g, NT)
        p_ref[at] = p
        a, b = fold(w, jnp.add), fold(w * p, jnp.add)
        total, dotted = (a, b) if total is None else (total + a, dotted + b)
    return top, jnp.sum(total, axis=0, keepdims=True), jnp.sum(dotted, axis=0, keepdims=True)


def gradients(qn, g, inverse, row_dot, knt_ref, w_ref, p_ref, key_acc, value_acc):
    query_t = None
    for c in range(0, w_ref.shape[0], CHUNK):
        at = pl.ds(c, CHUNK)
        probs = w_ref[at] * inverse
        value_acc[at] += dot(probs.astype(jnp.bfloat16), g)
        score_grad = (probs * (p_ref[at] - row_dot) * SCALE).astype(jnp.bfloat16)
        key_acc[at] += dot(score_grad, qn)
        part = dot(knt_ref[:, at], score_grad)
        query_t = part if query_t is None else query_t + part
    return query_t


def kernel(
    pairs, dps, factor,
    q_in, g_in, k_in, v_in, q_gain_in, k_gain_in,
    q_out, k_out, v_out, q_term, k_term,
    held, kept, ready, units, qn, kn, knt, w, p, key_acc, value_acc, own_part, part, their_part, tops, stats, their_stats, own_center, their_center, center_t, term, terms,
    q_gain, k_gain, gain_sem, there_send, there_recv, kept_send, kept_recv, own_sem, back_send, back_recv, back_own,
    part_send, part_recv, stats_send, stats_recv, center_send, center_recv, term_send, term_recv,
):
    me, group = lax.axis_index("seq"), lax.axis_index("dp")
    j, half = me // 2, lax.rem(me, 2)
    other = 1 - half
    turn = j // (pairs // BLOCKS)
    ins, outs = (q_in, g_in, k_in, v_in), (q_out, k_out, v_out)
    samples, tokens, _ = q_in.shape
    items = 2 * samples
    length = pairs * tokens
    span = length // BLOCKS
    mine = pl.ds(pl.multiple_of(j * tokens, tokens), tokens)
    partner = (group, 2 * j + other)

    def columns(i, pair):
        return pl.ds(pl.multiple_of((2 * pair + i % 2) * DEPTH, DEPTH), DEPTH)

    def rows_of(pair):
        return pl.ds(pl.multiple_of(pair * tokens, tokens), tokens)

    def there(i, t, side, pair):
        return pltpu.make_async_remote_copy(
            src_ref=ins[t].at[i // 2, :, columns(i, pair)], dst_ref=held.at[i, t, side, mine],
            send_sem=there_send.at[i, t, side], recv_sem=there_recv.at[i, t, side],
            device_id=(group, 2 * pair + (other if side else half)), device_id_type=MESH)

    def keep(i, t, pair):
        return pltpu.make_async_remote_copy(
            src_ref=ins[t + 2].at[i // 2, :, columns(i, pair)], dst_ref=kept.at[i, t, mine],
            send_sem=kept_send.at[i, t], recv_sem=kept_recv.at[i, t],
            device_id=(group, 2 * pair + half), device_id_type=MESH)

    def own(i, t):
        target = held.at[i, t, 0, mine] if t < 2 else kept.at[i, t - 2, mine]
        return pltpu.make_async_copy(ins[t].at[i // 2, :, columns(i, j)], target, own_sem.at[i, t])

    def back(i, o, pair):
        return pltpu.make_async_remote_copy(
            src_ref=ready.at[i, o, rows_of(pair)], dst_ref=outs[o].at[i // 2, :, columns(i, j)],
            send_sem=back_send.at[i, o], recv_sem=back_recv.at[i, o],
            device_id=(group, 2 * pair + half), device_id_type=MESH)

    def back_local(i, o):
        return pltpu.make_async_copy(ready.at[i, o, mine], outs[o].at[i // 2, :, columns(i, j)], back_own.at[i, o])

    def all_of(send, recv, count):
        rows = held.at[0, 0, 0, pl.ds(0, count * tokens)]
        return pltpu.make_async_remote_copy(
            src_ref=rows, dst_ref=rows, send_sem=send, recv_sem=recv, device_id=(group, me), device_id_type=MESH)

    def there_all(i, t, side):
        return all_of(there_send.at[i, t, side], there_recv.at[i, t, side], pairs if side else pairs - 1)

    def kept_all(i, t):
        return all_of(kept_send.at[i, t], kept_recv.at[i, t], pairs - 1)

    def back_all(i, o):
        return all_of(back_send.at[i, o], back_recv.at[i, o], pairs - 1)

    def send_back(i, o):
        back_local(i, o).start()

        @pl.loop(1, pairs, unroll=5)
        def _(r):
            back(i, o, lax.rem(j + r, pairs)).start()

    def send_part(i, n):
        at = pl.ds(pl.multiple_of(n * span, span), span)
        return pltpu.make_async_remote_copy(
            src_ref=part.at[i, at], dst_ref=their_part.at[i, at],
            send_sem=part_send.at[i, n], recv_sem=part_recv.at[i, n], device_id=partner, device_id_type=MESH)

    def send_stats(i):
        return pltpu.make_async_remote_copy(
            src_ref=stats.at[i], dst_ref=their_stats.at[i],
            send_sem=stats_send.at[i], recv_sem=stats_recv.at[i], device_id=partner, device_id_type=MESH)

    def send_center(i):
        return pltpu.make_async_remote_copy(
            src_ref=own_center.at[i], dst_ref=their_center.at[i],
            send_sem=center_send.at[i], recv_sem=center_recv.at[i], device_id=partner, device_id_type=MESH)

    def issue(i):
        for t in range(2):
            @pl.loop(0, pairs, unroll=4)
            def _(r):
                there(i, t, 1, lax.rem(j + r, pairs)).start()

        for t in range(2):
            @pl.loop(1, pairs, unroll=5)
            def _(r):
                keep(i, t, lax.rem(j + r, pairs)).start()

        for t in range(2):
            @pl.loop(1, pairs, unroll=5)
            def _(r):
                there(i, t, 0, lax.rem(j + r, pairs)).start()

    barrier = pltpu.get_barrier_semaphore()
    seq = 2 * pairs

    @pl.loop(1, seq, unroll=31)
    def _(r):
        pl.semaphore_signal(barrier, inc=1, device_id=(group, lax.rem(me + r, seq)), device_id_type=MESH)

    @pl.loop(1, dps, unroll=7)
    def _(r):
        for side in range(2):
            pl.semaphore_signal(
                barrier, inc=1, device_id=(lax.rem(group + r, dps), 2 * j + (other if side else half)),
                device_id_type=MESH)

    for i in range(items):
        for t in range(4):
            own(i, t).start()
    gains = [
        pltpu.make_async_copy(q_gain_in, q_gain, gain_sem.at[0]),
        pltpu.make_async_copy(k_gain_in, k_gain, gain_sem.at[1]),
    ]
    for copy in gains:
        copy.start()
    pl.semaphore_wait(barrier, seq - 1 + 2 * (dps - 1))
    issue(0)
    issue(1)
    issue(2)

    for copy in gains:
        copy.wait()
    gain_q = [q_gain[pl.ds(2 * j + e, 1)] for e in range(2)]
    gain_k = [k_gain[pl.ds(2 * j + e, 1)] for e in range(2)]
    term[...] = jnp.zeros_like(term)

    def first(i, side):
        slot, e = i % 2, i % 2

        @pl.loop(0, BLOCKS)
        def _(block):
            n, at = side * BLOCKS + block, pl.ds(pl.multiple_of(block * span, span), span)
            unit, _ = unit_of(held[i, 0, side, at])
            units[slot, side, at] = unit
            normed = (unit * gain_q[e]).astype(jnp.bfloat16)
            qn[slot, side, at] = normed
            top, total, dotted = weigh(
                normed, held[i, 1, side, at], kn.at[slot], kept.at[i, 1], w.at[slot, n], p.at[slot, n])
            tops[slot, pl.ds(n, 1)] = top
            stats[i, 0, pl.ds(n, 1)] = top + jnp.log2(total)
            stats[i, 1, pl.ds(n, 1)] = dotted / total

    def near(i):
        slot, e = i % 2, i % 2
        own(i, 2).wait()
        kept_all(i, 0).wait_recv()
        normalize(kept.at[i, 0], gain_k[e], kn.at[slot])
        knt[slot] = kn[slot].T
        mean = jnp.mean(kn[slot].astype(jnp.float32), axis=0, keepdims=True)
        own_center[i] = mean
        send_center(i).start()
        own(i, 3).wait()
        kept_all(i, 1).wait_recv()
        for t in range(2):
            own(i, t).wait()
            there_all(i, t, 0).wait_recv()
        first(i, 0)

    def send_parts(i):
        @pl.loop(0, BLOCKS)
        def _(n):
            send_part(i, lax.rem(n + turn, BLOCKS)).start()

    def far(i):
        for t in range(2):
            there_all(i, t, 1).wait_recv()
        first(i, 1)
        send_stats(i).start()
        if i + 3 < items:
            issue(i + 3)
        if i == items - 1:
            for past in range(1, items - 2):
                send_parts(past)

    def second(i):
        slot, e = i % 2, i % 2
        send_stats(i).wait_recv()
        send_center(i).wait_recv()
        for side, center in enumerate((their_center, own_center)):
            center_t[side] = jnp.broadcast_to(center[i], (BQ, DEPTH)).T
        key_acc[...] = jnp.zeros_like(key_acc)
        value_acc[...] = jnp.zeros_like(value_acc)

        @pl.loop(0, 2 * BLOCKS)
        def _(m):
            side, block = 1 - m // BLOCKS, lax.rem(m + turn, BLOCKS)
            n, theirs = side * BLOCKS + block, (1 - side) * BLOCKS + block
            at = pl.ds(pl.multiple_of(block * span, span), span)
            level, dotted = (stats[i, c, pl.ds(n, 1)] for c in range(2))
            their_level, their_dotted = (their_stats[i, c, pl.ds(theirs, 1)] for c in range(2))
            highest = jnp.maximum(level, their_level)
            here, away = jnp.exp2(level - highest), jnp.exp2(their_level - highest)
            inverse = 1.0 / (here + away)
            row_dot = (dotted * here + their_dotted * away) * inverse
            scale = jnp.exp2(tops[slot, pl.ds(n, 1)] - highest) * inverse
            gone = here * inverse * (row_dot - dotted) * SCALE
            back_in = away * inverse * (their_dotted - row_dot) * SCALE
            grad = gradients(
                qn[slot, side, at], held[i, 1, side, at], scale, row_dot,
                knt.at[slot], w.at[slot, n], p.at[slot, n], key_acc, value_acc)
            grad = (grad + center_t[side] * jnp.where(side == 1, gone, back_in)).T
            term[e, 0:1] += jnp.sum(grad * units[slot, side, at], axis=0, keepdims=True)

            @pl.when(side == 1)
            def _():
                part[i, at] = grad.astype(jnp.bfloat16)
                if i != 1:
                    send_part(i, block).start()

            @pl.when(side == 0)
            def _():
                own_part[i, at] = grad

        @pl.loop(0, BLOCKS)
        def _(n):
            at = pl.ds(pl.multiple_of(n * span, span), span)
            result, sums = norm_back(kept[i, 0, at], key_acc[at].astype(jnp.bfloat16), gain_k[e])
            ready[i, 1, at] = result
            term[e, 1:2] += sums
            ready[i, 2, at] = value_acc[at].astype(jnp.bfloat16)

        send_back(i, 1)
        send_back(i, 2)

    def last(i):
        e = i % 2

        @pl.loop(0, BLOCKS)
        def _(m):
            n = lax.rem(m + turn, BLOCKS)
            at = pl.ds(pl.multiple_of(n * span, span), span)
            send_part(i, n).wait_recv()
            grad = (own_part[i, at] + their_part[i, at].astype(jnp.float32)).astype(jnp.bfloat16)
            ready[i, 0, at], _ = norm_back(held[i, 0, 0, at], grad, gain_q[e])
            shift = span // tokens

            @pl.loop(0, shift)
            def _(r):
                pair = n * shift + r

                @pl.when(pair != j)
                def _():
                    back(i, 0, pair).start()

                @pl.when(pair == j)
                def _():
                    back_local(i, 0).start()

    near(0)
    far(0)
    near(1)
    far(1)
    for i in range(2, items):
        second(i - 2)
        near(i)
        far(i)
    second(items - 2)
    last(0)
    second(items - 1)
    def share(r, side):
        slot = 2 * r + side
        return pltpu.make_async_remote_copy(
            src_ref=term.at[other if side else half], dst_ref=terms.at[slot],
            send_sem=term_send.at[slot], recv_sem=term_recv.at[slot],
            device_id=(lax.rem(group + r, dps), 2 * j + (other if side else half)), device_id_type=MESH)

    shares = [(r, side) for r in range(dps) for side in range(2) if r or side]
    for r, side in shares:
        share(r, side).start()
    for i in range(1, items):
        last(i)
    for r, side in shares:
        share(r, side).wait()
    total = term[half]
    for r, side in shares:
        total += terms[2 * r + side]
    q_term[...] = total[0:1] * factor
    k_term[...] = total[1:2] * factor
    for i in range(items):
        send_stats(i).wait_send()
        send_center(i).wait_send()
        for n in range(BLOCKS):
            send_part(i, n).wait_send()
        for t in range(2):
            kept_all(i, t).wait_send()
            for side in range(2):
                there_all(i, t, side).wait_send()
        for o in range(3):
            back_local(i, o).wait()
            back_all(i, o).wait()


def hand_over(*refs):
    sems = refs[-1]
    copies = [pltpu.make_async_copy(src, dst, sems.at[c]) for c, (src, dst) in enumerate(zip(refs[:5], refs[5:10]))]
    for copy in copies:
        copy.start()
    for copy in copies:
        copy.wait()


def solution(mesh):
    seq, dps = mesh.shape["seq"], mesh.shape["dp"]
    pairs = seq // 2

    def step(queries, keys, values, out_grad, q_gain, k_gain):
        samples, tokens, _ = queries.shape
        items, length = 2 * samples, pairs * tokens
        assert length == BLOCKS * BQ
        vmem = pl.BlockSpec(memory_space=pltpu.VMEM)
        whole = jax.ShapeDtypeStruct(queries.shape, jnp.bfloat16)
        row = jax.ShapeDtypeStruct((1, DEPTH), jnp.float32)
        dma = pltpu.SemaphoreType.DMA
        low, wide = jnp.bfloat16, jnp.float32
        results = pl.pallas_call(
            functools.partial(kernel, pairs, dps, 1.0 / math.sqrt(samples * dps * seq * tokens)),
            out_shape=(pltpu.VMEM(whole.shape, low),) * 3 + (pltpu.VMEM(row.shape, wide),) * 2,
            in_specs=[pl.BlockSpec(memory_space=pltpu.HBM)] * 6,
            out_specs=[vmem] * 5,
            scratch_shapes=[
                pltpu.VMEM((items, 2, 2, length, DEPTH), low),
                pltpu.VMEM((items, 2, length, DEPTH), low),
                pltpu.VMEM((items, 3, length, DEPTH), low),
                pltpu.VMEM((2, 2, length, DEPTH), wide),
                pltpu.VMEM((2, 2, length, DEPTH), low),
                pltpu.VMEM((2, length, DEPTH), low),
                pltpu.VMEM((2, DEPTH, length), low),
                pltpu.VMEM((2, 2 * BLOCKS, length, BQ), wide),
                pltpu.VMEM((2, 2 * BLOCKS, length, BQ), wide),
                pltpu.VMEM((length, DEPTH), wide),
                pltpu.VMEM((length, DEPTH), wide),
                pltpu.VMEM((items, length, DEPTH), wide),
                pltpu.VMEM((items, length, DEPTH), low),
                pltpu.VMEM((items, length, DEPTH), low),
                pltpu.VMEM((2, 2 * BLOCKS, BQ), wide),
                pltpu.VMEM((items, 2, 2 * BLOCKS, BQ), wide),
                pltpu.VMEM((items, 2, 2 * BLOCKS, BQ), wide),
                pltpu.VMEM((items, 1, DEPTH), wide),
                pltpu.VMEM((items, 1, DEPTH), wide),
                pltpu.VMEM((2, DEPTH, BQ), wide),
                pltpu.VMEM((2, 2, DEPTH), wide),
                pltpu.VMEM((2 * dps, 2, DEPTH), wide),
                pltpu.VMEM(q_gain.shape, wide), pltpu.VMEM(k_gain.shape, wide), dma((2,)),
                dma((items, 2, 2)), dma((items, 2, 2)), dma((items, 2)), dma((items, 2)), dma((items, 4)),
                dma((items, 3)), dma((items, 3)), dma((items, 3)),
                dma((items, BLOCKS)), dma((items, BLOCKS)), dma((items,)), dma((items,)), dma((items,)), dma((items,)),
                dma((2 * dps,)), dma((2 * dps,)),
            ],
            compiler_params=pltpu.CompilerParams(
                collective_id=0, has_side_effects=True, vmem_limit_bytes=54 * 2**20
            ),
        )(queries, out_grad, keys, values, q_gain, k_gain)
        hbm = pl.BlockSpec(memory_space=pltpu.HBM)
        return pl.pallas_call(
            hand_over,
            out_shape=(pltpu.HBM(whole.shape, low),) * 3 + (pltpu.HBM(row.shape, wide),) * 2,
            in_specs=[vmem] * 5,
            out_specs=[hbm] * 5,
            scratch_shapes=[dma((5,))],
        )(*(pltpu.with_memory_space_constraint(x, pltpu.VMEM) for x in results))

    return jax.shard_map(
        step,
        mesh=mesh,
        in_specs=(P("dp", "seq", None),) * 4 + (P(), P()),
        out_specs=(P("dp", "seq", None),) * 3 + (P("seq", None),) * 2,
        check_vma=False,
    )
```
